512 devices in a mesh: seg: 16 (over y, core), vid: 16 (over z, x_hi), tp: 2 (over x_lo).
Axes of the slice: x: 4 (x_hi: 2, x_lo: 2; x = x_hi * 2 + x_lo), y: 8, z: 8, core: 2. Of those that a mesh axis runs over, the one named last changes fastest.
Arguments:
- tokens: bfloat16 [16, 8192, 2048], P('vid', 'seg', 'tp'), may hold values from -400 to 400
- key_weight: bfloat16 [2048, 2048], P('vid', 'tp'), may hold values from -0.125 to 0.125
- query_weight: bfloat16 [2048, 2048], P('vid', 'tp'), may hold values from -0.125 to 0.125
- latent_queries: bfloat16 [128, 2048], P(None, 'tp'), may hold values from -400 to 400
- init_memory: float32 [16, 128, 2048], P('vid', None, 'tp'), may hold values from -6 to 6
- forget: float32 [16, 16, 2048], P('vid', 'seg', 'tp'), may hold values from 0 to 1
Outputs:
- mixed: bfloat16 [16, 8192, 2048], P('vid', 'seg', 'tp')
- memory: float32 [16, 2048, 2048], P('vid', 'seg', 'tp')
The draws below stay inside these ranges and needn't reach their ends.
All inputs are finite; a program needn't handle non-finite values.
Results may differ from the reference program's by a relative error of at most 0.015.
The reference program's roundings to bfloat16 on the way count: a program that leaves them out, or rounds other values in their place, can miss the bound.
Values may be sent and summed in bfloat16 or wider, within the bound.
No kernel may reach another device: no remote copies, remote signals or barrier semaphores. Data moves between devices by JAX's collectives and lax.ppermute only.
A program may use at most 64 MiB of HBM per device.

```python
import jax
import jax.numpy as jnp
from jax import lax

D = 2048
HEAD = 128
M = 128
TOK = 512
HEADS = 16
SEGMENT_COUNT = 16
VIDEO_COUNT = 16
FRAMES = 8192


def draw_tokens(key, part):
    base = jax.random.normal(jax.random.fold_in(key, 11), (VIDEO_COUNT, FRAMES, D), jnp.float32)
    return jnp.clip(base, -400.0, 400.0).astype(jnp.bfloat16)


def draw_latent_queries(key, part):
    base = jax.random.normal(jax.random.fold_in(key, 21), (M, D), jnp.float32)
    return jnp.clip(base, -400.0, 400.0).astype(jnp.bfloat16)


def draw_forget(key, part):
    slow = 0.1 ** (1.0 / SEGMENT_COUNT)
    low = 0.02
    level = jax.random.uniform(jax.random.fold_in(key, 31), (VIDEO_COUNT, 1, D), jnp.float32)
    rate = jnp.exp(jnp.log(low) + level * (jnp.log(slow) - jnp.log(low)))
    power = jax.random.uniform(jax.random.fold_in(key, 32), (VIDEO_COUNT, SEGMENT_COUNT, D), jnp.float32, 0.5, 1.0)
    retained_memory = rate ** power
    segment_group = jax.random.randint(jax.random.fold_in(key, 33), (VIDEO_COUNT, SEGMENT_COUNT, 1), 0, 6) == 0
    training_loss = jax.random.uniform(jax.random.fold_in(key, 34), (VIDEO_COUNT, SEGMENT_COUNT, 1), jnp.float32, 0.5, 0.8)
    return retained_memory * jnp.where(segment_group, training_loss, 1.0)


def steps_of(stream_key, shape, pieces, smallest, largest):
    gain = 1.0
    for axis_at, parts in pieces:
        heights = jax.random.uniform(jax.random.fold_in(jax.random.fold_in(stream_key, 6), axis_at), (parts,), jnp.float32, smallest / len(pieces), largest / len(pieces))
        gain = gain * jnp.repeat(jnp.exp(heights), shape[axis_at] // parts).reshape((-1,) + (1,) * (len(shape) - 1 - axis_at))
    return gain


def bell_draw(key, shape, deviation, bound, split=(), held_as=jnp.bfloat16):
    result = deviation * jax.random.normal(key, shape, jnp.float32)
    if split:
        result = result * steps_of(key, shape, split, -0.22, 0.18)
    return jnp.clip(result, -bound, bound).astype(held_as)


def setup_inputs(seed: int = 0) -> dict:
    splits = jax.random.split(jax.random.key(seed), 7)
    tokens = draw_tokens(jax.random.fold_in(splits[6], 71), 0)
    key_weight = bell_draw(splits[1], (D, D), D ** -0.5, 0.125, ((0, 16), (1, 2)))
    query_weight = bell_draw(splits[2], (D, D), D ** -0.5, 0.125, ((0, 16), (1, 2)))
    latent_queries = draw_latent_queries(jax.random.fold_in(splits[6], 71), 0)
    init_memory = bell_draw(splits[4], (VIDEO_COUNT, M, D), 1.0, 6.0, ((0, 16), (2, 2)), jnp.float32)
    forget = draw_forget(jax.random.fold_in(splits[6], 71), 0)
    return dict(tokens=tokens, key_weight=key_weight, query_weight=query_weight, latent_queries=latent_queries, init_memory=init_memory, forget=forget)


def rounded(value):
    return lax.optimization_barrier(value.astype(jnp.bfloat16)).astype(jnp.float32)

def trailing_softmax(scores):
    top = lax.optimization_barrier(jnp.max(scores, axis=-1, keepdims=True))
    expo = jnp.exp(scores - top)
    return expo / lax.optimization_barrier(jnp.sum(expo, axis=-1, keepdims=True))

def resample(latent, keys, values):
    scores = jnp.einsum('mhe,the->hmt', latent, keys) / jnp.sqrt(jnp.float32(HEAD))
    weight_params = rounded(trailing_softmax(scores))
    return jnp.einsum('hmt,the->mhe', weight_params, values)

def readout(queries, memory_in):
    heads = memory_in.reshape(M, HEADS, HEAD)
    normed = heads * lax.rsqrt(lax.optimization_barrier(jnp.mean(heads * heads, axis=-1, keepdims=True)) + 1e-06)
    scores = jnp.einsum('the,mhe->htm', queries, rounded(normed)) / jnp.sqrt(jnp.float32(HEAD))
    weight_params = rounded(trailing_softmax(scores))
    return jnp.einsum('htm,mhe->the', weight_params, rounded(heads))

def reference(tokens, key_weight, query_weight, latent_queries, init_memory, forget):
    latent = latent_queries.astype(jnp.float32).reshape(M, HEADS, HEAD)

    def video(items):
        frames, initial_memory, retain = items
        keys = jnp.dot(frames, key_weight, preferred_element_type=jnp.float32).astype(jnp.bfloat16).astype(jnp.float32)
        queries = jnp.dot(frames, query_weight, preferred_element_type=jnp.float32).astype(jnp.bfloat16).astype(jnp.float32)
        keys = keys.reshape(SEGMENT_COUNT, TOK, HEADS, HEAD)
        queries = queries.reshape(SEGMENT_COUNT, TOK, HEADS, HEAD)
        values = frames.astype(jnp.float32).reshape(SEGMENT_COUNT, TOK, HEADS, HEAD)

        def step(memory_in, segment):
            seg_keys, seg_queries, seg_values, seg_retain = segment
            update = resample(latent, seg_keys, seg_values).reshape(M, D)
            read = readout(seg_queries, memory_in).reshape(TOK, D)
            mixed = (seg_values.reshape(TOK, D) + read).astype(jnp.bfloat16)
            memory_out = seg_retain[None, :] * memory_in + update
            return (memory_out, (mixed, memory_out))
        last, (mixed, memory) = lax.scan(step, initial_memory, (keys, queries, values, retain))
        return (mixed.reshape(FRAMES, D), memory.reshape(SEGMENT_COUNT * M, D))
    return lax.map(video, (tokens, init_memory, forget))
```

```python
import jax
import jax.numpy as jnp
from jax import lax
from jax.experimental import pallas as pl
from jax.experimental.pallas import tpu as pltpu
from jax.sharding import Mesh, PartitionSpec as P

HEAD = 128
M = 128
TOK = 512
HALF = 1024
QUART = 512
Y, C, Z, H, L = 8, 2, 8, 2, 2
AXES = ("y", "c", "z", "h", "l")
BF = jnp.bfloat16
F32 = jnp.float32
SCALE = 128.0**-0.5
VMEM = pl.BlockSpec(memory_space=pltpu.VMEM)
PARAMS = pltpu.CompilerParams(vmem_limit_bytes=40 * 1024 * 1024)


def rank(y, c, z, h, l):
    return (((y * C + c) * Z + z) * H + h) * L + l


def sent(x, move):
    pairs = []
    for y in range(Y):
        for c in range(C):
            for z in range(Z):
                for h in range(H):
                    for l in range(L):
                        pairs.append((rank(y, c, z, h, l), rank(*move(y, c, z, h, l))))
    return lax.ppermute(x, AXES, pairs)


def to_core(x):
    return sent(x, lambda y, c, z, h, l: (y, 1 - c, z, h, l))


def to_tp(x):
    return sent(x, lambda y, c, z, h, l: (y, c, z, h, 1 - l))


def to_h(x):
    return sent(x, lambda y, c, z, h, l: (y, c, z, 1 - h, l))


def to_y(x, d):
    return sent(x, lambda y, c, z, h, l: ((y + d) % Y, c, z, h, l))


def to_z(x, d):
    return sent(x, lambda y, c, z, h, l: (y, c, (z + d) % Z, h, l))


def softmax(s):
    top = jnp.max(s, axis=-1, keepdims=True)
    e = jnp.exp(s - top)
    return (e / jnp.sum(e, axis=-1, keepdims=True)).astype(BF)


def dot(a, b):
    return jnp.dot(a, b, preferred_element_type=F32)


def dot_t(a, b):
    return lax.dot_general(a, b, (((1,), (1,)), ((), ())), preferred_element_type=F32)


def lanes(block, width):
    return pl.ds(pl.multiple_of(block * width, width), width)


def update_kernel(ml, mr, ol, orr, s0, s1, s2a, s2b, s3, lat, fm, fo, u_ref, p_ref, w):
    y, c, z, l = (lax.axis_index(a) for a in ("y", "c", "z", "l"))
    k = lax.rem(y + 2 * z, 4)
    w[:, lanes(k, HEAD)] = s0[...]
    w[:, lanes(lax.rem(k + 1, 4), HEAD)] = s1[...]
    w[0:HALF, lanes(lax.rem(k + 2, 4), HEAD)] = s2a[...]
    w[HALF:, lanes(lax.rem(k + 2, 4), HEAD)] = s2b[...]
    w[:, lanes(lax.rem(k + 3, 4), HEAD)] = s3[...]
    for j, (a, b) in enumerate(((ml, mr), (ol, orr))):
        keys = (
            dot(a[...], w[lanes(l, HALF), :]) + dot(b[...], w[lanes(1 - l, HALF), :])
        ).astype(BF)
        for h in range(4):
            cols = pl.ds(pl.multiple_of(c * QUART + h * HEAD, HEAD), HEAD)
            wts = softmax(dot_t(lat[:, cols], keys[:, h * HEAD : (h + 1) * HEAD]) * SCALE)
            u_ref[j, :, h * HEAD : (h + 1) * HEAD] = dot(wts, a[:, cols])
    mine, other = fm[:, lanes(c, QUART)], fo[:, lanes(c, QUART)]
    first = c == 0
    f1 = jnp.where(first, other, mine)
    u0 = jnp.where(first, u_ref[0], u_ref[1])
    u1 = jnp.where(first, u_ref[1], u_ref[0])
    p_ref[:, 0:16, :] = (f1 * u0 + u1).astype(BF).reshape(Y, 16, QUART)
    f = mine * other
    hi = f.astype(BF)
    rest = f - hi.astype(F32)
    mid = rest.astype(BF)
    low = (rest - mid.astype(F32)).astype(BF)
    row = lax.broadcasted_iota(jnp.int32, (16, QUART), 0)
    rows = jnp.where(
        row == 0,
        hi.astype(F32),
        jnp.where(row == 1, mid.astype(F32), jnp.where(row == 2, low.astype(F32), 0.0)),
    ).astype(BF)
    p_ref[:, 16:32, :] = jnp.broadcast_to(rows[None], (Y, 16, QUART))


def scan_kernel(p, init, e_ref):
    y, c = lax.axis_index("y"), lax.axis_index("c")
    e = init[pl.ds(pl.multiple_of(y * 16, 16), 16), lanes(c, QUART)]
    for s in range(Y):
        e_ref[s] = e.astype(BF)
        rows = p[s, 16:32, :].astype(F32)
        f = rows[0:1] + rows[1:2] + rows[2:3]
        e = f * e + p[s, 0:16, :].astype(F32)


def query_kernel(ml, mr, ol, orr, w, q_ref):
    l = lax.axis_index("l")
    for j, (a, b) in enumerate(((ml, mr), (ol, orr))):
        q_ref[j] = (
            dot(a[...], w[lanes(l, HALF), :]) + dot(b[...], w[lanes(1 - l, HALF), :])
        ).astype(BF)


def read_kernel(tok, qm, qo, em, eo, um, uo, fm, fo, mixed, mem):
    c = lax.axis_index("c")
    first = c == 0
    f0 = jnp.where(first, fm[...], fo[...])
    for half, (q, e, u) in enumerate(((qm, em, um), (qo, eo, uo))):
        part = c if half == 0 else 1 - c
        at = lanes(part, QUART)
        g = jnp.where(first, fm[:, at], fo[:, at])
        mine = fm[:, at]
        own, oth = (u[0], u[1]) if half == 0 else (u[1], u[0])
        e0 = e[...].astype(F32)
        entering = jnp.where(first, e0, g * e0 + oth)
        mem[:, at] = mine * entering + own
        for h in range(4):
            lo = h * HEAD
            x = entering[:, lo : lo + HEAD]
            keys = (x * lax.rsqrt(jnp.mean(x * x, axis=-1, keepdims=True) + 1e-6)).astype(BF)
            wts = softmax(dot_t(q[:, lo : lo + HEAD], keys) * SCALE)
            r = dot(wts, x.astype(BF))
            cols = pl.ds(pl.multiple_of(part * QUART + lo, HEAD), HEAD)
            mixed[:, cols] = (tok[:, cols].astype(F32) + r).astype(BF)


def shards(tokens, key_weight, query_weight, latent_queries, init_memory, forget):
    y, c, z, h = (lax.axis_index(a) for a in ("y", "c", "z", "h"))
    mine_l = tokens[0]
    fm = forget[0]
    mine_r = to_tp(mine_l)
    qw = lax.dynamic_slice(query_weight, (0, c * QUART), (128, QUART))
    qw2 = to_h(qw)
    both = jnp.stack([jnp.where(h == 0, qw, qw2), jnp.where(h == 0, qw2, qw)])
    wq = lax.all_gather(both[None], "z", tiled=True).reshape(2048, QUART)
    even = lax.dynamic_slice(key_weight, (0, c * QUART + (y % 4) * HEAD), (128, HEAD))
    odd = lax.dynamic_slice(key_weight, (0, c * QUART + ((y + 2) % 4) * HEAD), (128, HEAD))
    out = jnp.stack([even, even, odd, odd] * 4)
    s0 = lax.all_to_all(out, ("z", "h"), 0, 0, tiled=True).reshape(2048, HEAD)
    s1 = to_y(s0, -1)
    s3 = to_y(s0, 1)
    s2a = to_z(s0[:HALF], 1)
    s2b = to_z(s0[HALF:], -1)
    other_l = to_core(mine_l)
    fo = to_core(fm)
    other_r = to_core(mine_r)
    u, packed = pl.pallas_call(
        update_kernel,
        out_shape=(
            jax.ShapeDtypeStruct((2, M, QUART), F32),
            jax.ShapeDtypeStruct((Y, 32, QUART), BF),
        ),
        in_specs=[VMEM] * 12,
        out_specs=(VMEM, VMEM),
        scratch_shapes=[pltpu.VMEM((2048, QUART), BF)],
        compiler_params=PARAMS,
        cost_estimate=pl.CostEstimate(
            flops=2 * 1024 * 2048 * 512, bytes_accessed=7 << 20, transcendentals=1 << 19
        ),
        name="update",
    )(mine_l, mine_r, other_l, other_r, s0, s1, s2a, s2b, s3, latent_queries, fm, fo)
    arrived = lax.all_to_all(packed, "y", 0, 0, tiled=True)
    u_other = to_core(u)
    queries = pl.pallas_call(
        query_kernel,
        out_shape=jax.ShapeDtypeStruct((2, TOK, QUART), BF),
        in_specs=[VMEM] * 5,
        out_specs=VMEM,
        compiler_params=PARAMS,
        cost_estimate=pl.CostEstimate(
            flops=2 * 1024 * 2048 * 512, bytes_accessed=7 << 20, transcendentals=0
        ),
        name="query",
    )(mine_l, mine_r, other_l, other_r, wq)
    q_other = to_core(queries[1])
    entered = pl.pallas_call(
        scan_kernel,
        out_shape=jax.ShapeDtypeStruct((Y, 16, QUART), BF),
        in_specs=[VMEM] * 2,
        out_specs=VMEM,
        compiler_params=PARAMS,
        name="scan",
    )(arrived, init_memory[0])
    e = lax.all_to_all(entered, "y", 0, 0, tiled=True).reshape(M, QUART)
    e_other = to_core(e)
    mixed, mem = pl.pallas_call(
        read_kernel,
        out_shape=(
            jax.ShapeDtypeStruct((TOK, HALF), BF),
            jax.ShapeDtypeStruct((M, HALF), F32),
        ),
        in_specs=[VMEM] * 9,
        out_specs=(VMEM, VMEM),
        compiler_params=PARAMS,
        name="read",
    )(mine_l, queries[0], q_other, e, e_other, u, u_other, fm, fo)
    return mixed[None], mem[None]


def solution(mesh):
    fine = Mesh(mesh.devices.reshape(Y, C, Z, H, L), AXES)
    seg, vid = ("y", "c"), ("z", "h")
    return jax.shard_map(
        shards,
        mesh=fine,
        in_specs=(
            P(vid, seg, "l"),
            P(vid, "l"),
            P(vid, "l"),
            P(None, "l"),
            P(vid, None, "l"),
            P(vid, seg, "l"),
        ),
        out_specs=(P(vid, seg, "l"), P(vid, seg, "l")),
        check_vma=False,
    )
```

```python
import jax
import jax.numpy as jnp
from jax import lax
from jax.experimental import pallas as pl
from jax.experimental.pallas import tpu as pltpu
from jax.sharding import Mesh, PartitionSpec as P

HEAD = 128
M = 128
TOK = 512
HALF = 1024
QUART = 512
Y, C, Z, H, L = 8, 2, 8, 2, 2
AXES = ("y", "c", "z", "h", "l")
BF = jnp.bfloat16
F32 = jnp.float32
SCALE = 128.0**-0.5
VMEM = pl.BlockSpec(memory_space=pltpu.VMEM)
PARAMS = pltpu.CompilerParams(vmem_limit_bytes=24 * 1024 * 1024)


def rank(y, c, z, h, l):
    return (((y * C + c) * Z + z) * H + h) * L + l


def sent(x, move):
    pairs = []
    for y in range(Y):
        for c in range(C):
            for z in range(Z):
                for h in range(H):
                    for l in range(L):
                        pairs.append((rank(y, c, z, h, l), rank(*move(y, c, z, h, l))))
    return lax.ppermute(x, AXES, pairs)


def to_core(x):
    return sent(x, lambda y, c, z, h, l: (y, 1 - c, z, h, l))


def to_tp(x):
    return sent(x, lambda y, c, z, h, l: (y, c, z, h, 1 - l))


def to_h(x):
    return sent(x, lambda y, c, z, h, l: (y, c, z, 1 - h, l))


def to_y(x, d):
    return sent(x, lambda y, c, z, h, l: ((y + d) % Y, c, z, h, l))


def to_z(x, d):
    return sent(x, lambda y, c, z, h, l: (y, c, (z + d) % Z, h, l))


def softmax(s):
    top = jnp.max(s, axis=-1, keepdims=True)
    e = jnp.exp(s - top)
    return (e / jnp.sum(e, axis=-1, keepdims=True)).astype(BF)


def dot(a, b):
    return jnp.dot(a, b, preferred_element_type=F32)


def dot_t(a, b):
    return lax.dot_general(a, b, (((1,), (1,)), ((), ())), preferred_element_type=F32)


def lanes(block, width):
    return pl.ds(pl.multiple_of(block * width, width), width)


def resample(a, b, w, lat, u_ref):
    c, l = lax.axis_index("c"), lax.axis_index("l")
    keys = (
        dot(a[...], w[lanes(l, HALF), :]) + dot(b[...], w[lanes(1 - l, HALF), :])
    ).astype(BF)
    for h in range(4):
        cols = pl.ds(pl.multiple_of(c * QUART + h * HEAD, HEAD), HEAD)
        wts = softmax(dot_t(lat[:, cols], keys[:, h * HEAD : (h + 1) * HEAD]) * SCALE)
        u_ref[:, h * HEAD : (h + 1) * HEAD] = dot(wts, a[:, cols])


def first_kernel(a, b, s0, s1, s2a, s2b, s3, lat, u_ref, w):
    y, z = lax.axis_index("y"), lax.axis_index("z")
    k = lax.rem(y + 2 * z, 4)
    w[:, lanes(k, HEAD)] = s0[...]
    w[:, lanes(lax.rem(k + 1, 4), HEAD)] = s1[...]
    w[0:HALF, lanes(lax.rem(k + 2, 4), HEAD)] = s2a[...]
    w[HALF:, lanes(lax.rem(k + 2, 4), HEAD)] = s2b[...]
    w[:, lanes(lax.rem(k + 3, 4), HEAD)] = s3[...]
    resample(a, b, w, lat, u_ref)


def second_kernel(a, b, w, lat, um, fm, fo, u_ref, p_ref):
    c = lax.axis_index("c")
    u_ref[0] = um[...]
    resample(a, b, w, lat, u_ref.at[1])
    mine, other = fm[:, lanes(c, QUART)], fo[:, lanes(c, QUART)]
    first = c == 0
    f1 = jnp.where(first, other, mine)
    u0 = jnp.where(first, u_ref[0], u_ref[1])
    u1 = jnp.where(first, u_ref[1], u_ref[0])
    p_ref[:, :, 0:QUART] = (f1 * u0 + u1).astype(BF).reshape(Y, 16, QUART)
    f = mine * other
    hi = f.astype(BF)
    rest = f - hi.astype(F32)
    mid = rest.astype(BF)
    low = (rest - mid.astype(F32)).astype(BF)
    terms = [
        t.astype(F32)[:, i * HEAD : (i + 1) * HEAD] for t in (hi, mid, low) for i in range(4)
    ]
    rows = jnp.concatenate(terms + [jnp.zeros((4, HEAD), F32)], axis=0).astype(BF)
    p_ref[:, :, QUART:] = jnp.broadcast_to(rows[None], (Y, 16, HEAD))


def scan_kernel(p, init, e_ref):
    y, c = lax.axis_index("y"), lax.axis_index("c")
    e = init[pl.ds(pl.multiple_of(y * 16, 16), 16), lanes(c, QUART)]
    for s in range(Y):
        e_ref[s] = e.astype(BF)
        rows = p[s, :, QUART:].astype(F32)
        rows = rows[0:4] + rows[4:8] + rows[8:12]
        f = jnp.concatenate([rows[i : i + 1] for i in range(4)], axis=1)
        e = f * e + p[s, :, 0:QUART].astype(F32)


def query_kernel(ml, mr, ol, orr, t0, t1a, t1b, qm_ref, qo_ref, w):
    l, z = lax.axis_index("l"), lax.axis_index("z")
    k = lax.rem(z, 2)
    w[:, lanes(k, 256)] = t0[...]
    w[0:HALF, lanes(1 - k, 256)] = t1a[...]
    w[HALF:, lanes(1 - k, 256)] = t1b[...]
    for q_ref, a, b in ((qm_ref, ml, mr), (qo_ref, ol, orr)):
        q_ref[...] = (
            dot(a[...], w[lanes(l, HALF), :]) + dot(b[...], w[lanes(1 - l, HALF), :])
        ).astype(BF)


def read_kernel(tok, qm, qo, em, eo, um, uo, fm, fo, mixed, mem):
    c = lax.axis_index("c")
    first = c == 0
    f0 = jnp.where(first, fm[...], fo[...])
    for half, (q, e, u) in enumerate(((qm, em, um), (qo, eo, uo))):
        part = c if half == 0 else 1 - c
        at = lanes(part, QUART)
        g = jnp.where(first, fm[:, at], fo[:, at])
        mine = fm[:, at]
        own, oth = (u[0], u[1]) if half == 0 else (u[1], u[0])
        e0 = e[...].astype(F32)
        entering = jnp.where(first, e0, g * e0 + oth)
        mem[:, at] = mine * entering + own
        for h in range(4):
            lo = h * HEAD
            x = entering[:, lo : lo + HEAD]
            keys = (x * lax.rsqrt(jnp.mean(x * x, axis=-1, keepdims=True) + 1e-6)).astype(BF)
            wts = softmax(dot_t(q[:, lo : lo + HEAD], keys) * SCALE)
            r = dot(wts, x.astype(BF))
            cols = pl.ds(pl.multiple_of(part * QUART + lo, HEAD), HEAD)
            mixed[:, cols] = (tok[:, cols].astype(F32) + r).astype(BF)


def spread(pair):
    wide = jnp.stack(pair)[None, :, None]
    return jnp.broadcast_to(wide, (4, 2, 2, *pair[0].shape)).reshape(16, *pair[0].shape)


def shards(tokens, key_weight, query_weight, latent_queries, init_memory, forget):
    y, c, z, h = (lax.axis_index(a) for a in ("y", "c", "z", "h"))
    tie = lax.optimization_barrier
    fm = forget[0]
    even = lax.dynamic_slice(key_weight, (0, c * QUART + (y % 4) * HEAD), (128, HEAD))
    odd = lax.dynamic_slice(key_weight, (0, c * QUART + ((y + 2) % 4) * HEAD), (128, HEAD))
    qeven = lax.dynamic_slice(query_weight, (0, c * QUART), (128, 256))
    qodd = lax.dynamic_slice(query_weight, (0, c * QUART + 256), (128, 256))
    out, mine_l = tie((spread((even, odd)), tokens[0]))
    s0 = lax.all_to_all(out, ("z", "h"), 0, 0, tiled=True).reshape(2048, HEAD)
    mine_r = to_tp(mine_l)
    other_l = to_core(mine_l)
    fo = to_core(fm)
    qout, fo = tie((spread((qeven, qodd)), fo))
    t0 = lax.all_to_all(qout, ("z", "h"), 0, 0, tiled=True).reshape(2048, 256)
    s0, fo, other_l = tie((s0, fo, other_l))
    s1 = to_y(s0, -1)
    s3 = to_y(s0, 1)
    s2a = to_z(s0[:HALF], 1)
    s2b = to_z(s0[HALF:], -1)
    s1, s3, s2a, s2b, mine_r = tie((s1, s3, s2a, s2b, mine_r))
    other_r = to_core(mine_r)
    cost = pl.CostEstimate(
        flops=2 * 512 * 2048 * 512, bytes_accessed=7 << 20, transcendentals=1 << 18
    )
    um, w = pl.pallas_call(
        first_kernel,
        out_shape=(
            jax.ShapeDtypeStruct((M, QUART), F32),
            jax.ShapeDtypeStruct((2048, QUART), BF),
        ),
        in_specs=[VMEM] * 8,
        out_specs=(VMEM, VMEM),
        compiler_params=PARAMS,
        cost_estimate=cost,
        name="first",
    )(mine_l, mine_r, s0, s1, s2a, s2b, s3, latent_queries)
    u, packed = pl.pallas_call(
        second_kernel,
        out_shape=(
            jax.ShapeDtypeStruct((2, M, QUART), F32),
            jax.ShapeDtypeStruct((Y, 16, QUART + HEAD), BF),
        ),
        in_specs=[VMEM] * 7,
        out_specs=(VMEM, VMEM),
        compiler_params=PARAMS,
        cost_estimate=cost,
        name="second",
    )(other_l, other_r, w, latent_queries, um, fm, fo)
    arrived = lax.all_to_all(packed, "y", 0, 0, tiled=True)
    packed, t0 = tie((packed, t0))
    t1a = to_z(t0[:HALF], 1)
    t1b = to_z(t0[HALF:], -1)
    swapped = to_core(u)
    entered = pl.pallas_call(
        scan_kernel,
        out_shape=jax.ShapeDtypeStruct((Y, 16, QUART), BF),
        in_specs=[VMEM] * 2,
        out_specs=VMEM,
        compiler_params=PARAMS,
        name="scan",
    )(arrived, init_memory[0])
    entered, t0 = tie((entered, t0))
    queries = pl.pallas_call(
        query_kernel,
        out_shape=(jax.ShapeDtypeStruct((TOK, QUART), BF),) * 2,
        in_specs=[VMEM] * 7,
        out_specs=(VMEM, VMEM),
        scratch_shapes=[pltpu.VMEM((2048, QUART), BF)],
        compiler_params=PARAMS,
        cost_estimate=pl.CostEstimate(
            flops=2 * 1024 * 2048 * 512, bytes_accessed=7 << 20, transcendentals=0
        ),
        name="query",
    )(mine_l, mine_r, other_l, other_r, t0, t1a, t1b)
    e = lax.all_to_all(entered, "y", 0, 0, tiled=True).reshape(M, QUART)
    e_other = to_core(e)
    q_late, e_late = tie((queries[1], e))
    q_other = to_core(q_late)
    mixed, mem = pl.pallas_call(
        read_kernel,
        out_shape=(
            jax.ShapeDtypeStruct((TOK, HALF), BF),
            jax.ShapeDtypeStruct((M, HALF), F32),
        ),
        in_specs=[VMEM] * 9,
        out_specs=(VMEM, VMEM),
        compiler_params=PARAMS,
        name="read",
    )(mine_l, queries[0], q_other, e, e_other, u, swapped, fm, fo)
    return mixed[None], mem[None]


def solution(mesh):
    fine = Mesh(mesh.devices.reshape(Y, C, Z, H, L), AXES)
    seg, vid = ("y", "c"), ("z", "h")
    return jax.shard_map(
        shards,
        mesh=fine,
        in_specs=(
            P(vid, seg, "l"),
            P(vid, "l"),
            P(vid, "l"),
            P(None, "l"),
            P(vid, None, "l"),
            P(vid, seg, "l"),
        ),
        out_specs=(P(vid, seg, "l"), P(vid, seg, "l")),
        check_vma=False,
    )
```

```python
import jax
import jax.numpy as jnp
from jax import lax
from jax.experimental import pallas as pl
from jax.experimental.pallas import tpu as pltpu
from jax.sharding import Mesh, PartitionSpec as P

HEAD = 128
M = 128
TOK = 512
HALF = 1024
QUART = 512
Y, C, Z, H, L = 8, 2, 8, 2, 2
AXES = ("y", "c", "z", "h", "l")
BF = jnp.bfloat16
F32 = jnp.float32
SCALE = 128.0**-0.5
SCAN_COST = 1 << 20
KERNEL_COST = 1024
VMEM = pl.BlockSpec(memory_space=pltpu.VMEM)
ANY = pl.BlockSpec(memory_space=pltpu.HBM)
PARAMS = pltpu.CompilerParams(vmem_limit_bytes=24 * 1024 * 1024)


def rank(y, c, z, h, l):
    return (((y * C + c) * Z + z) * H + h) * L + l


def sent(x, move):
    pairs = []
    for y in range(Y):
        for c in range(C):
            for z in range(Z):
                for h in range(H):
                    for l in range(L):
                        pairs.append((rank(y, c, z, h, l), rank(*move(y, c, z, h, l))))
    return lax.ppermute(x, AXES, pairs)


def to_core(x):
    return sent(x, lambda y, c, z, h, l: (y, 1 - c, z, h, l))


def to_tp(x):
    return sent(x, lambda y, c, z, h, l: (y, c, z, h, 1 - l))


def to_h(x):
    return sent(x, lambda y, c, z, h, l: (y, c, z, 1 - h, l))


def to_y(x, d):
    return sent(x, lambda y, c, z, h, l: ((y + d) % Y, c, z, h, l))


def to_z(x, d):
    return sent(x, lambda y, c, z, h, l: (y, c, (z + d) % Z, h, l))


def softmax(s):
    top = jnp.max(s, axis=-1, keepdims=True)
    e = jnp.exp(s - top)
    return (e / jnp.sum(e, axis=-1, keepdims=True)).astype(BF)


def dot(a, b):
    return jnp.dot(a, b, preferred_element_type=F32)


def dot_t(a, b):
    return lax.dot_general(a, b, (((1,), (1,)), ((), ())), preferred_element_type=F32)


def lanes(block, width):
    return pl.ds(pl.multiple_of(block * width, width), width)


def fetch(pairs, sems):
    copies = [pltpu.make_async_copy(a, b, sems.at[i]) for i, (a, b) in enumerate(pairs)]
    for copy in copies:
        copy.start()
    return copies


def columns_of(w, slabs):
    k = lax.rem(lax.axis_index("y") + 2 * lax.axis_index("z"), 4)
    return [(s, w.at[:, lanes(lax.rem(k + i, 4), HEAD)]) for i, s in enumerate(slabs)]


def projected(a, b, w, later):
    l = lax.axis_index("l")
    left = dot(a[...], w[lanes(l, HALF), :])
    later.wait()
    return (left + dot(b[...], w[lanes(1 - l, HALF), :])).astype(BF)


def resample(a_in, b_in, s0, s1, s2, s3, lat, u_ref, w, a, b, sems):
    c = lax.axis_index("c")
    copies = fetch(columns_of(w, (s0, s1, s2, s3)) + [(a_in, a), (b_in, b)], sems)
    for copy in copies[:5]:
        copy.wait()
    keys = projected(a, b, w, copies[5])
    for h in range(4):
        cols = pl.ds(pl.multiple_of(c * QUART + h * HEAD, HEAD), HEAD)
        wts = softmax(dot_t(lat[:, cols], keys[:, h * HEAD : (h + 1) * HEAD]) * SCALE)
        u_ref[:, h * HEAD : (h + 1) * HEAD] = dot(wts, a[:, cols])


def second_kernel(
    a_in, b_in, s0, s1, s2, s3, lat, um, fm, fo, u_out, p_out, w, a, b, sems, u_ref, p_ref
):
    c = lax.axis_index("c")
    u_ref[0] = um[...]
    resample(a_in, b_in, s0, s1, s2, s3, lat, u_ref.at[1], w, a, b, sems)
    mine, other = fm[:, lanes(c, QUART)], fo[:, lanes(c, QUART)]
    first = c == 0
    f1 = jnp.where(first, other, mine)
    u0 = jnp.where(first, u_ref[0], u_ref[1])
    u1 = jnp.where(first, u_ref[1], u_ref[0])
    p_ref[:, :, 0:QUART] = (f1 * u0 + u1).astype(BF).reshape(Y, 16, QUART)
    f = mine * other
    hi = f.astype(BF)
    rest = f - hi.astype(F32)
    mid = rest.astype(BF)
    low = (rest - mid.astype(F32)).astype(BF)
    terms = [
        t.astype(F32)[:, i * HEAD : (i + 1) * HEAD] for t in (hi, mid, low) for i in range(4)
    ]
    rows = jnp.concatenate(terms + [jnp.zeros((4, HEAD), F32)], axis=0).astype(BF)
    p_ref[:, :, QUART:] = jnp.broadcast_to(rows[None], (Y, 16, HEAD))
    for copy in fetch([(p_ref, p_out), (u_ref, u_out)], sems):
        copy.wait()


def scan_kernel(p, init_in, e_ref, init, sem):
    y, c = lax.axis_index("y"), lax.axis_index("c")
    rows = pl.ds(pl.multiple_of(y * 16, 16), 16)
    (copy,) = fetch([(init_in.at[rows, lanes(c, QUART)], init)], sem)
    copy.wait()
    e = init[...]
    for s in range(Y):
        e_ref[s] = e.astype(BF)
        rows = p[s, :, QUART:].astype(F32)
        rows = rows[0:4] + rows[4:8] + rows[8:12]
        f = jnp.concatenate([rows[i : i + 1] for i in range(4)], axis=1)
        e = f * e + p[s, :, 0:QUART].astype(F32)


def query_kernel(
    ml_in, mr_in, ol_in, or_in, t0, t1, t2, t3, qm_out, qo_out, w, ml, mr, ol, orr, qm, qo, sems
):
    rest = [(ol_in, ol), (or_in, orr), (ml_in, ml), (mr_in, mr)]
    copies = fetch(columns_of(w, (t0, t1, t2, t3)) + rest, sems)
    for copy in copies[:5]:
        copy.wait()
    qo[...] = projected(ol, orr, w, copies[5])
    (out_o,) = fetch([(qo, qo_out)], sems)
    copies[6].wait()
    qm[...] = projected(ml, mr, w, copies[7])
    (out_m,) = fetch([(qm, qm_out)], sems.at[pl.ds(1, 1)])
    out_o.wait()
    out_m.wait()


def read_kernel(
    tok_in, qm_in, qo_in, um_in, uo_in, em, eo, fm, fo, mixed, mem, tok, qm, qo, um, uo, sems
):
    copies = fetch([(um_in, um), (qm_in, qm), (tok_in, tok), (uo_in, uo), (qo_in, qo)], sems)
    c = lax.axis_index("c")
    first = c == 0
    f0 = jnp.where(first, fm[...], fo[...])
    for half, (q, e, u) in enumerate(((qm, em, um), (qo, eo, uo))):
        part = c if half == 0 else 1 - c
        at = lanes(part, QUART)
        g = jnp.where(first, fm[:, at], fo[:, at])
        mine = fm[:, at]
        copies[3 * half].wait()
        own, oth = (u[0], u[1]) if half == 0 else (u[1], u[0])
        e0 = e[...].astype(F32)
        entering = jnp.where(first, e0, g * e0 + oth)
        mem[:, at] = mine * entering + own
        copies[3 * half + 1].wait()
        if half == 0:
            copies[2].wait()
        for h in range(4):
            lo = h * HEAD
            x = entering[:, lo : lo + HEAD]
            keys = (x * lax.rsqrt(jnp.mean(x * x, axis=-1, keepdims=True) + 1e-6)).astype(BF)
            wts = softmax(dot_t(q[:, lo : lo + HEAD], keys) * SCALE)
            r = dot(wts, x.astype(BF))
            cols = pl.ds(pl.multiple_of(part * QUART + lo, HEAD), HEAD)
            mixed[:, cols] = (tok[:, cols].astype(F32) + r).astype(BF)


def spread(pair):
    wide = jnp.stack(pair)[None, :, None]
    return jnp.broadcast_to(wide, (4, 2, 2, *pair[0].shape)).reshape(16, *pair[0].shape)


def split_kernel(both, k_out, q_out, sems):
    pairs = [(both.at[:, 0:HEAD], k_out), (both.at[:, HEAD : 2 * HEAD], q_out)]
    for copy in fetch(pairs, sems):
        copy.wait()


def head_columns(a, b, at):
    parts = [lax.dynamic_slice(x, (0, at), (128, HEAD)) for x in (a, b)]
    return jnp.concatenate(parts, axis=1)


def shards(tokens, key_weight, query_weight, latent_queries, init_memory, forget):
    y, c, z, h = (lax.axis_index(a) for a in ("y", "c", "z", "h"))
    tie = lax.optimization_barrier
    fm = forget[0]
    even = head_columns(key_weight, query_weight, c * QUART + (y % 4) * HEAD)
    odd = head_columns(key_weight, query_weight, c * QUART + ((y + 2) % 4) * HEAD)
    out, mine_l = tie((spread((even, odd)), tokens[0]))
    both = lax.all_to_all(out, ("z", "h"), 0, 0, tiled=True).reshape(2048, 2 * HEAD)
    mine_r = to_tp(mine_l)
    other_l = to_core(mine_l)
    fo = to_core(fm)
    both, fo, other_l = tie((both, fo, other_l))
    s0, t0 = pl.pallas_call(
        split_kernel,
        out_shape=(jax.ShapeDtypeStruct((2048, HEAD), BF),) * 2,
        in_specs=[ANY],
        out_specs=(ANY, ANY),
        scratch_shapes=[pltpu.SemaphoreType.DMA((2,))],
        compiler_params=PARAMS,
        name="split",
    )(both)
    s1 = to_y(s0, -1)
    s3 = to_y(s0, 1)
    s2 = to_z(s0, 1)
    t1 = to_y(t0, -1)
    t3 = to_y(t0, 1)
    t2 = to_z(t0, -1)
    other_r = to_core(mine_r)
    cost = pl.CostEstimate(
        flops=KERNEL_COST, bytes_accessed=KERNEL_COST, transcendentals=0
    )
    scratch = [
        pltpu.VMEM((2048, QUART), BF),
        pltpu.VMEM((TOK, HALF), BF),
        pltpu.VMEM((TOK, HALF), BF),
        pltpu.SemaphoreType.DMA((6,)),
    ]
    um = pl.pallas_call(
        resample,
        out_shape=jax.ShapeDtypeStruct((M, QUART), F32),
        in_specs=[ANY] * 6 + [VMEM],
        out_specs=VMEM,
        scratch_shapes=scratch,
        compiler_params=PARAMS,
        cost_estimate=cost,
        name="first",
    )(mine_l, mine_r, s0, s1, s2, s3, latent_queries)
    u, packed = pl.pallas_call(
        second_kernel,
        out_shape=(
            jax.ShapeDtypeStruct((2, M, QUART), F32),
            jax.ShapeDtypeStruct((Y, 16, QUART + HEAD), BF),
        ),
        in_specs=[ANY] * 6 + [VMEM] * 4,
        out_specs=(ANY, ANY),
        scratch_shapes=scratch
        + [
            pltpu.VMEM((2, M, QUART), F32),
            pltpu.VMEM((Y, 16, QUART + HEAD), BF),
        ],
        compiler_params=PARAMS,
        cost_estimate=cost,
        name="second",
    )(other_l, other_r, s0, s1, s2, s3, latent_queries, um, fm, fo)
    arrived = lax.all_to_all(packed, "y", 0, 0, tiled=True)
    swapped = to_core(u)
    entered = pl.pallas_call(
        scan_kernel,
        out_shape=jax.ShapeDtypeStruct((Y, 16, QUART), BF),
        in_specs=[VMEM, ANY],
        out_specs=VMEM,
        scratch_shapes=[pltpu.VMEM((16, QUART), F32), pltpu.SemaphoreType.DMA((1,))],
        compiler_params=PARAMS,
        cost_estimate=pl.CostEstimate(
            flops=SCAN_COST, bytes_accessed=1 << 20, transcendentals=0
        ),
        name="scan",
    )(arrived, init_memory[0])
    queries = pl.pallas_call(
        query_kernel,
        out_shape=(jax.ShapeDtypeStruct((TOK, QUART), BF),) * 2,
        in_specs=[ANY] * 8,
        out_specs=(ANY, ANY),
        scratch_shapes=[pltpu.VMEM((2048, QUART), BF)]
        + [pltpu.VMEM((TOK, HALF), BF)] * 4
        + [pltpu.VMEM((TOK, QUART), BF)] * 2
        + [pltpu.SemaphoreType.DMA((8,))],
        compiler_params=PARAMS,
        cost_estimate=pl.CostEstimate(
            flops=2 * 1024 * 2048 * 512, bytes_accessed=7 << 20, transcendentals=0
        ),
        name="query",
    )(mine_l, mine_r, other_l, other_r, t0, t1, t2, t3)
    e = lax.all_to_all(entered, "y", 0, 0, tiled=True).reshape(M, QUART)
    e_other = to_core(e)
    q_other = to_core(queries[1])
    mixed, mem = pl.pallas_call(
        read_kernel,
        out_shape=(
            jax.ShapeDtypeStruct((TOK, HALF), BF),
            jax.ShapeDtypeStruct((M, HALF), F32),
        ),
        in_specs=[ANY] * 5 + [VMEM] * 4,
        out_specs=(VMEM, VMEM),
        scratch_shapes=[
            pltpu.VMEM((TOK, HALF), BF),
            pltpu.VMEM((TOK, QUART), BF),
            pltpu.VMEM((TOK, QUART), BF),
            pltpu.VMEM((2, M, QUART), F32),
            pltpu.VMEM((2, M, QUART), F32),
            pltpu.SemaphoreType.DMA((5,)),
        ],
        compiler_params=PARAMS,
        name="read",
    )(mine_l, queries[0], q_other, u, swapped, e, e_other, fm, fo)
    return mixed[None], mem[None]


def solution(mesh):
    fine = Mesh(mesh.devices.reshape(Y, C, Z, H, L), AXES)
    seg, vid = ("y", "c"), ("z", "h")
    return jax.shard_map(
        shards,
        mesh=fine,
        in_specs=(
            P(vid, seg, "l"),
            P(vid, "l"),
            P(vid, "l"),
            P(None, "l"),
            P(vid, None, "l"),
            P(vid, seg, "l"),
        ),
        out_specs=(P(vid, seg, "l"), P(vid, seg, "l")),
        check_vma=False,
    )
```

```python
import jax
import jax.numpy as jnp
from jax import lax
from jax.experimental import pallas as pl
from jax.experimental.pallas import tpu as pltpu
from jax.sharding import Mesh, PartitionSpec as P

HEAD = 128
M = 128
TOK = 512
HALF = 1024
QUART = 512
Y, C, Z, H, L = 8, 2, 8, 2, 2
AXES = ("y", "c", "z", "h", "l")
BF = jnp.bfloat16
F32 = jnp.float32
SCALE = 128.0**-0.5
SCAN_COST = 50 * 10**9
KERNEL_COST = 1024
VMEM = pl.BlockSpec(memory_space=pltpu.VMEM)
ANY = pl.BlockSpec(memory_space=pltpu.HBM)
PARAMS = pltpu.CompilerParams(vmem_limit_bytes=24 * 1024 * 1024)


def rank(y, c, z, h, l):
    return (((y * C + c) * Z + z) * H + h) * L + l


def sent(x, move):
    pairs = []
    for y in range(Y):
        for c in range(C):
            for z in range(Z):
                for h in range(H):
                    for l in range(L):
                        pairs.append((rank(y, c, z, h, l), rank(*move(y, c, z, h, l))))
    return lax.ppermute(x, AXES, pairs)


def to_core(x):
    return sent(x, lambda y, c, z, h, l: (y, 1 - c, z, h, l))


def to_tp(x):
    return sent(x, lambda y, c, z, h, l: (y, c, z, h, 1 - l))


def to_h(x):
    return sent(x, lambda y, c, z, h, l: (y, c, z, 1 - h, l))


def to_y(x, d):
    return sent(x, lambda y, c, z, h, l: ((y + d) % Y, c, z, h, l))


def to_z(x, d):
    return sent(x, lambda y, c, z, h, l: (y, c, (z + d) % Z, h, l))


def softmax(s):
    top = jnp.max(s, axis=-1, keepdims=True)
    e = jnp.exp(s - top)
    return (e / jnp.sum(e, axis=-1, keepdims=True)).astype(BF)


def dot(a, b):
    return jnp.dot(a, b, preferred_element_type=F32)


def dot_t(a, b):
    return lax.dot_general(a, b, (((1,), (1,)), ((), ())), preferred_element_type=F32)


def lanes(block, width):
    return pl.ds(pl.multiple_of(block * width, width), width)


def fetch(pairs, sems):
    copies = [pltpu.make_async_copy(a, b, sems.at[i]) for i, (a, b) in enumerate(pairs)]
    for copy in copies:
        copy.start()
    return copies


def columns_of(w, slabs):
    k = lax.rem(lax.axis_index("y") + 2 * lax.axis_index("z"), 4)
    return [(s, w.at[:, lanes(lax.rem(k + i, 4), HEAD)]) for i, s in enumerate(slabs)]


def projected(a, b, w, later):
    l = lax.axis_index("l")
    left = dot(a[...], w[lanes(l, HALF), :])
    later.wait()
    return (left + dot(b[...], w[lanes(1 - l, HALF), :])).astype(BF)


def resample(a_in, b_in, s0, s1, s2, s3, lat, u_ref, w, a, b, sems):
    c = lax.axis_index("c")
    copies = fetch(columns_of(w, (s0, s1, s2, s3)) + [(a_in, a), (b_in, b)], sems)
    for copy in copies[:5]:
        copy.wait()
    keys = projected(a, b, w, copies[5])
    for h in range(4):
        cols = pl.ds(pl.multiple_of(c * QUART + h * HEAD, HEAD), HEAD)
        wts = softmax(dot_t(lat[:, cols], keys[:, h * HEAD : (h + 1) * HEAD]) * SCALE)
        u_ref[:, h * HEAD : (h + 1) * HEAD] = dot(wts, a[:, cols])


def second_kernel(
    a_in, b_in, s0, s1, s2, s3, lat, um, fm, fo, u_out, p_out, w, a, b, sems, u_ref, p_ref
):
    c = lax.axis_index("c")
    u_ref[0] = um[...]
    resample(a_in, b_in, s0, s1, s2, s3, lat, u_ref.at[1], w, a, b, sems)
    mine, other = fm[:, lanes(c, QUART)], fo[:, lanes(c, QUART)]
    first = c == 0
    f1 = jnp.where(first, other, mine)
    u0 = jnp.where(first, u_ref[0], u_ref[1])
    u1 = jnp.where(first, u_ref[1], u_ref[0])
    p_ref[:, :, 0:QUART] = (f1 * u0 + u1).astype(BF).reshape(Y, 16, QUART)
    f = mine * other
    hi = f.astype(BF)
    rest = f - hi.astype(F32)
    mid = rest.astype(BF)
    low = (rest - mid.astype(F32)).astype(BF)
    terms = [
        t.astype(F32)[:, i * HEAD : (i + 1) * HEAD] for t in (hi, mid, low) for i in range(4)
    ]
    rows = jnp.concatenate(terms + [jnp.zeros((4, HEAD), F32)], axis=0).astype(BF)
    p_ref[:, :, QUART:] = jnp.broadcast_to(rows[None], (Y, 16, HEAD))
    for copy in fetch([(p_ref, p_out), (u_ref, u_out)], sems):
        copy.wait()


def scan_kernel(p, init_in, e_ref, init, sem):
    y, c = lax.axis_index("y"), lax.axis_index("c")
    rows = pl.ds(pl.multiple_of(y * 16, 16), 16)
    (copy,) = fetch([(init_in.at[rows, lanes(c, QUART)], init)], sem)
    copy.wait()
    e = init[...]
    for s in range(Y):
        e_ref[s] = e.astype(BF)
        rows = p[s, :, QUART:].astype(F32)
        rows = rows[0:4] + rows[4:8] + rows[8:12]
        f = jnp.concatenate([rows[i : i + 1] for i in range(4)], axis=1)
        e = f * e + p[s, :, 0:QUART].astype(F32)


def query_kernel(
    ml_in, mr_in, ol_in, or_in, t0, t1, t2, t3, qm_out, qo_out, w, ml, mr, ol, orr, qm, qo, sems
):
    rest = [(ol_in, ol), (or_in, orr), (ml_in, ml), (mr_in, mr)]
    copies = fetch(columns_of(w, (t0, t1, t2, t3)) + rest, sems)
    for copy in copies[:5]:
        copy.wait()
    qo[...] = projected(ol, orr, w, copies[5])
    (out_o,) = fetch([(qo, qo_out)], sems)
    copies[6].wait()
    qm[...] = projected(ml, mr, w, copies[7])
    (out_m,) = fetch([(qm, qm_out)], sems.at[pl.ds(1, 1)])
    out_o.wait()
    out_m.wait()


def read_kernel(
    tok_in, qm_in, qo_in, um_in, uo_in, em, eo, fm, fo, mixed, mem, tok, qm, qo, um, uo, sems
):
    copies = fetch([(um_in, um), (qm_in, qm), (tok_in, tok), (uo_in, uo), (qo_in, qo)], sems)
    c = lax.axis_index("c")
    first = c == 0
    f0 = jnp.where(first, fm[...], fo[...])
    for half, (q, e, u) in enumerate(((qm, em, um), (qo, eo, uo))):
        part = c if half == 0 else 1 - c
        at = lanes(part, QUART)
        g = jnp.where(first, fm[:, at], fo[:, at])
        mine = fm[:, at]
        copies[3 * half].wait()
        own, oth = (u[0], u[1]) if half == 0 else (u[1], u[0])
        e0 = e[...].astype(F32)
        entering = jnp.where(first, e0, g * e0 + oth)
        mem[:, at] = mine * entering + own
        copies[3 * half + 1].wait()
        if half == 0:
            copies[2].wait()
        for h in range(4):
            lo = h * HEAD
            x = entering[:, lo : lo + HEAD]
            keys = (x * lax.rsqrt(jnp.mean(x * x, axis=-1, keepdims=True) + 1e-6)).astype(BF)
            wts = softmax(dot_t(q[:, lo : lo + HEAD], keys) * SCALE)
            r = dot(wts, x.astype(BF))
            cols = pl.ds(pl.multiple_of(part * QUART + lo, HEAD), HEAD)
            mixed[:, cols] = (tok[:, cols].astype(F32) + r).astype(BF)


def in_hbm(*arrays):
    return [pltpu.with_memory_space_constraint(a, pltpu.HBM) for a in arrays]


def spread(pair):
    wide = jnp.stack(pair)[None, :, None]
    return jnp.broadcast_to(wide, (4, 2, 2, *pair[0].shape)).reshape(16, *pair[0].shape)


def split_kernel(both, k_out, q_out, sems):
    pairs = [(both.at[:, 0:HEAD], k_out), (both.at[:, HEAD : 2 * HEAD], q_out)]
    for copy in fetch(pairs, sems):
        copy.wait()


def head_columns(a, b, at):
    parts = [lax.dynamic_slice(x, (0, at), (128, HEAD)) for x in (a, b)]
    return jnp.concatenate(parts, axis=1)


def shards(tokens, key_weight, query_weight, latent_queries, init_memory, forget):
    y, c, z, h = (lax.axis_index(a) for a in ("y", "c", "z", "h"))
    tie = lax.optimization_barrier
    fm = forget[0]
    even = head_columns(key_weight, query_weight, c * QUART + (y % 4) * HEAD)
    odd = head_columns(key_weight, query_weight, c * QUART + ((y + 2) % 4) * HEAD)
    out, mine_l = tie((spread((even, odd)), tokens[0]))
    both = lax.all_to_all(out, ("z", "h"), 0, 0, tiled=True).reshape(2048, 2 * HEAD)
    mine_r = to_tp(mine_l)
    other_l = to_core(mine_l)
    both, other_l = tie((both, other_l))
    s0, t0 = pl.pallas_call(
        split_kernel,
        out_shape=(jax.ShapeDtypeStruct((2048, HEAD), BF),) * 2,
        in_specs=[ANY],
        out_specs=(ANY, ANY),
        scratch_shapes=[pltpu.SemaphoreType.DMA((2,))],
        compiler_params=PARAMS,
        name="split",
    )(both)
    s1 = to_y(s0, -1)
    s3 = to_y(s0, 1)
    s2 = to_z(s0, 1)
    fm, _ = tie((fm, s0))
    fo = to_core(fm)
    s1, s3, s2, fo, mine_r = tie((s1, s3, s2, fo, mine_r))
    other_r = to_core(mine_r)
    cost = pl.CostEstimate(
        flops=KERNEL_COST, bytes_accessed=KERNEL_COST, transcendentals=0
    )
    scratch = [
        pltpu.VMEM((2048, QUART), BF),
        pltpu.VMEM((TOK, HALF), BF),
        pltpu.VMEM((TOK, HALF), BF),
        pltpu.SemaphoreType.DMA((6,)),
    ]
    um = pl.pallas_call(
        resample,
        out_shape=jax.ShapeDtypeStruct((M, QUART), F32),
        in_specs=[ANY] * 6 + [VMEM],
        out_specs=VMEM,
        scratch_shapes=scratch,
        compiler_params=PARAMS,
        cost_estimate=cost,
        name="first",
    )(mine_l, mine_r, s0, s1, s2, s3, latent_queries)
    u, packed = pl.pallas_call(
        second_kernel,
        out_shape=(
            pltpu.HBM((2, M, QUART), F32),
            pltpu.HBM((Y, 16, QUART + HEAD), BF),
        ),
        in_specs=[ANY] * 6 + [VMEM] * 4,
        out_specs=(ANY, ANY),
        scratch_shapes=scratch
        + [
            pltpu.VMEM((2, M, QUART), F32),
            pltpu.VMEM((Y, 16, QUART + HEAD), BF),
        ],
        compiler_params=PARAMS,
        cost_estimate=cost,
        name="second",
    )(other_l, other_r, s0, s1, s2, s3, latent_queries, um, fm, fo)
    arrived = lax.all_to_all(packed, "y", 0, 0, tiled=True)
    packed, t0 = tie((packed, t0))
    t1 = to_y(t0, -1)
    t3 = to_y(t0, 1)
    t2 = to_z(t0, -1)
    swapped = to_core(u)
    entered = pl.pallas_call(
        scan_kernel,
        out_shape=jax.ShapeDtypeStruct((Y, 16, QUART), BF),
        in_specs=[VMEM, ANY],
        out_specs=VMEM,
        scratch_shapes=[pltpu.VMEM((16, QUART), F32), pltpu.SemaphoreType.DMA((1,))],
        compiler_params=PARAMS,
        cost_estimate=pl.CostEstimate(
            flops=SCAN_COST, bytes_accessed=1 << 20, transcendentals=0
        ),
        name="scan",
    )(arrived, *in_hbm(init_memory[0]))
    entered, t0 = tie((entered, t0))
    queries = pl.pallas_call(
        query_kernel,
        out_shape=(pltpu.HBM((TOK, QUART), BF),) * 2,
        in_specs=[ANY] * 8,
        out_specs=(ANY, ANY),
        scratch_shapes=[pltpu.VMEM((2048, QUART), BF)]
        + [pltpu.VMEM((TOK, HALF), BF)] * 4
        + [pltpu.VMEM((TOK, QUART), BF)] * 2
        + [pltpu.SemaphoreType.DMA((8,))],
        compiler_params=PARAMS,
        cost_estimate=pl.CostEstimate(
            flops=2 * 1024 * 2048 * 512, bytes_accessed=7 << 20, transcendentals=0
        ),
        name="query",
    )(*in_hbm(mine_l, mine_r, other_l, other_r), t0, t1, t2, t3)
    e = lax.all_to_all(entered, "y", 0, 0, tiled=True).reshape(M, QUART)
    e_other = to_core(e)
    q_late, e_late = tie((queries[1], e))
    q_other = to_core(q_late)
    mixed, mem = pl.pallas_call(
        read_kernel,
        out_shape=(
            jax.ShapeDtypeStruct((TOK, HALF), BF),
            jax.ShapeDtypeStruct((M, HALF), F32),
        ),
        in_specs=[ANY] * 5 + [VMEM] * 4,
        out_specs=(VMEM, VMEM),
        scratch_shapes=[
            pltpu.VMEM((TOK, HALF), BF),
            pltpu.VMEM((TOK, QUART), BF),
            pltpu.VMEM((TOK, QUART), BF),
            pltpu.VMEM((2, M, QUART), F32),
            pltpu.VMEM((2, M, QUART), F32),
            pltpu.SemaphoreType.DMA((5,)),
        ],
        compiler_params=PARAMS,
        name="read",
    )(*in_hbm(mine_l, queries[0]), q_other, *in_hbm(u), swapped, e, e_other, fm, fo)
    return mixed[None], mem[None]


def solution(mesh):
    fine = Mesh(mesh.devices.reshape(Y, C, Z, H, L), AXES)
    seg, vid = ("y", "c"), ("z", "h")
    return jax.shard_map(
        shards,
        mesh=fine,
        in_specs=(
            P(vid, seg, "l"),
            P(vid, "l"),
            P(vid, "l"),
            P(None, "l"),
            P(vid, None, "l"),
            P(vid, seg, "l"),
        ),
        out_specs=(P(vid, seg, "l"), P(vid, seg, "l")),
        check_vma=False,
    )
```

```python
import jax
import jax.numpy as jnp
from jax import lax
from jax.experimental import pallas as pl
from jax.experimental.pallas import tpu as pltpu
from jax.sharding import Mesh, PartitionSpec as P

HEAD = 128
M = 128
TOK = 512
HALF = 1024
QUART = 512
Y, C, Z, H, L = 8, 2, 8, 2, 2
AXES = ("y", "c", "z", "h", "l")
BF = jnp.bfloat16
F32 = jnp.float32
SCALE = 128.0**-0.5
SCAN_COST = 50 * 10**9
KERNEL_COST = 1024
VMEM = pl.BlockSpec(memory_space=pltpu.VMEM)
ANY = pl.BlockSpec(memory_space=pltpu.HBM)
PARAMS = pltpu.CompilerParams(vmem_limit_bytes=24 * 1024 * 1024)


def rank(y, c, z, h, l):
    return (((y * C + c) * Z + z) * H + h) * L + l


def sent(x, move):
    pairs = []
    for y in range(Y):
        for c in range(C):
            for z in range(Z):
                for h in range(H):
                    for l in range(L):
                        pairs.append((rank(y, c, z, h, l), rank(*move(y, c, z, h, l))))
    return lax.ppermute(x, AXES, pairs)


def to_core(x):
    return sent(x, lambda y, c, z, h, l: (y, 1 - c, z, h, l))


def to_tp(x):
    return sent(x, lambda y, c, z, h, l: (y, c, z, h, 1 - l))


def to_h(x):
    return sent(x, lambda y, c, z, h, l: (y, c, z, 1 - h, l))


def to_y(x, d):
    return sent(x, lambda y, c, z, h, l: ((y + d) % Y, c, z, h, l))


def to_z(x, d):
    return sent(x, lambda y, c, z, h, l: (y, c, (z + d) % Z, h, l))


def softmax(s):
    top = jnp.max(s, axis=-1, keepdims=True)
    e = jnp.exp(s - top)
    return (e / jnp.sum(e, axis=-1, keepdims=True)).astype(BF)


def dot(a, b):
    return jnp.dot(a, b, preferred_element_type=F32)


def dot_t(a, b):
    return lax.dot_general(a, b, (((1,), (1,)), ((), ())), preferred_element_type=F32)


def lanes(block, width):
    return pl.ds(pl.multiple_of(block * width, width), width)


def fetch(pairs, sems):
    copies = [pltpu.make_async_copy(a, b, sems.at[i]) for i, (a, b) in enumerate(pairs)]
    for copy in copies:
        copy.start()
    return copies


def columns_of(w, slabs):
    k = lax.rem(lax.axis_index("y") + 2 * lax.axis_index("z"), 4)
    return [(s, w.at[:, lanes(lax.rem(k + i, 4), HEAD)]) for i, s in enumerate(slabs)]


def projected(a, b, w, later):
    l = lax.axis_index("l")
    left = dot(a[...], w[lanes(l, HALF), :])
    later.wait()
    return (left + dot(b[...], w[lanes(1 - l, HALF), :])).astype(BF)


def resample(a_in, b_in, s0, s1, s2, s3, lat, u_ref, w, a, b, sems):
    c = lax.axis_index("c")
    copies = fetch(columns_of(w, (s0, s1, s2, s3)) + [(a_in, a), (b_in, b)], sems)
    for copy in copies[:5]:
        copy.wait()
    keys = projected(a, b, w, copies[5])
    for h in range(4):
        cols = pl.ds(pl.multiple_of(c * QUART + h * HEAD, HEAD), HEAD)
        wts = softmax(dot_t(lat[:, cols], keys[:, h * HEAD : (h + 1) * HEAD]) * SCALE)
        u_ref[:, h * HEAD : (h + 1) * HEAD] = dot(wts, a[:, cols])


def second_kernel(
    a_in, b_in, s0, s1, s2, s3, lat, um, fm, fo, u_out, p_out, w, a, b, sems, u_ref, p_ref
):
    c = lax.axis_index("c")
    u_ref[0] = um[...]
    resample(a_in, b_in, s0, s1, s2, s3, lat, u_ref.at[1], w, a, b, sems)
    mine, other = fm[:, lanes(c, QUART)], fo[:, lanes(c, QUART)]
    first = c == 0
    f1 = jnp.where(first, other, mine)
    u0 = jnp.where(first, u_ref[0], u_ref[1])
    u1 = jnp.where(first, u_ref[1], u_ref[0])
    p_ref[:, :, 0:QUART] = (f1 * u0 + u1).astype(BF).reshape(Y, 16, QUART)
    f = mine * other
    hi = f.astype(BF)
    rest = f - hi.astype(F32)
    mid = rest.astype(BF)
    low = (rest - mid.astype(F32)).astype(BF)
    terms = [
        t.astype(F32)[:, i * HEAD : (i + 1) * HEAD] for t in (hi, mid, low) for i in range(4)
    ]
    rows = jnp.concatenate(terms + [jnp.zeros((4, HEAD), F32)], axis=0).astype(BF)
    p_ref[:, :, QUART:] = jnp.broadcast_to(rows[None], (Y, 16, HEAD))
    for copy in fetch([(p_ref, p_out), (u_ref, u_out)], sems):
        copy.wait()


def scan_kernel(p, init_in, e_ref, init, sem):
    y, c = lax.axis_index("y"), lax.axis_index("c")
    rows = pl.ds(pl.multiple_of(y * 16, 16), 16)
    (copy,) = fetch([(init_in.at[rows, lanes(c, QUART)], init)], sem)
    copy.wait()
    e = init[...]
    for s in range(Y):
        e_ref[s] = e.astype(BF)
        rows = p[s, :, QUART:].astype(F32)
        rows = rows[0:4] + rows[4:8] + rows[8:12]
        f = jnp.concatenate([rows[i : i + 1] for i in range(4)], axis=1)
        e = f * e + p[s, :, 0:QUART].astype(F32)


def query_kernel(
    ml_in, mr_in, ol_in, or_in, t0, t1, t3, t2, qm_out, qo_out, w, ml, mr, ol, orr, qm, qo, sems
):
    rest = [(ol_in, ol), (or_in, orr), (ml_in, ml), (mr_in, mr)]
    copies = fetch(columns_of(w, (t0, t1, t2, t3)) + rest, sems)
    for copy in copies[:5]:
        copy.wait()
    qo[...] = projected(ol, orr, w, copies[5])
    (out_o,) = fetch([(qo, qo_out)], sems)
    copies[6].wait()
    qm[...] = projected(ml, mr, w, copies[7])
    (out_m,) = fetch([(qm, qm_out)], sems.at[pl.ds(1, 1)])
    out_o.wait()
    out_m.wait()


def read_kernel(
    tok_in, qm_in, qo_in, um_in, uo_in, em, eo, fm, fo, mixed, mem, tok, qm, qo, um, uo, sems
):
    copies = fetch([(um_in, um), (qm_in, qm), (tok_in, tok), (uo_in, uo), (qo_in, qo)], sems)
    c = lax.axis_index("c")
    first = c == 0
    f0 = jnp.where(first, fm[...], fo[...])
    for half, (q, e, u) in enumerate(((qm, em, um), (qo, eo, uo))):
        part = c if half == 0 else 1 - c
        at = lanes(part, QUART)
        g = jnp.where(first, fm[:, at], fo[:, at])
        mine = fm[:, at]
        copies[3 * half].wait()
        own, oth = (u[0], u[1]) if half == 0 else (u[1], u[0])
        e0 = e[...].astype(F32)
        entering = jnp.where(first, e0, g * e0 + oth)
        mem[:, at] = mine * entering + own
        copies[3 * half + 1].wait()
        if half == 0:
            copies[2].wait()
        for h in range(4):
            lo = h * HEAD
            x = entering[:, lo : lo + HEAD]
            keys = (x * lax.rsqrt(jnp.mean(x * x, axis=-1, keepdims=True) + 1e-6)).astype(BF)
            wts = softmax(dot_t(q[:, lo : lo + HEAD], keys) * SCALE)
            r = dot(wts, x.astype(BF))
            cols = pl.ds(pl.multiple_of(part * QUART + lo, HEAD), HEAD)
            mixed[:, cols] = (tok[:, cols].astype(F32) + r).astype(BF)


def in_hbm(*arrays):
    return [pltpu.with_memory_space_constraint(a, pltpu.HBM) for a in arrays]


def spread(pair):
    wide = jnp.stack(pair)[None, :, None]
    return jnp.broadcast_to(wide, (4, 2, 2, *pair[0].shape)).reshape(16, *pair[0].shape)


def split_kernel(both, k_out, q_out, sems):
    pairs = [(both.at[:, 0:HEAD], k_out), (both.at[:, HEAD : 2 * HEAD], q_out)]
    for copy in fetch(pairs, sems):
        copy.wait()


def head_columns(a, b, at):
    parts = [lax.dynamic_slice(x, (0, at), (128, HEAD)) for x in (a, b)]
    return jnp.concatenate(parts, axis=1)


def shards(tokens, key_weight, query_weight, latent_queries, init_memory, forget):
    y, c, z, h = (lax.axis_index(a) for a in ("y", "c", "z", "h"))
    tie = lax.optimization_barrier
    fm = forget[0]
    even = head_columns(key_weight, query_weight, c * QUART + (y % 4) * HEAD)
    odd = head_columns(key_weight, query_weight, c * QUART + ((y + 2) % 4) * HEAD)
    out, mine_l = tie((spread((even, odd)), tokens[0]))
    both = lax.all_to_all(out, ("z", "h"), 0, 0, tiled=True).reshape(2048, 2 * HEAD)
    mine_r = to_tp(mine_l)
    other_l = to_core(mine_l)
    both, other_l = tie((both, other_l))
    s0, t0 = pl.pallas_call(
        split_kernel,
        out_shape=(jax.ShapeDtypeStruct((2048, HEAD), BF),) * 2,
        in_specs=[ANY],
        out_specs=(ANY, ANY),
        scratch_shapes=[pltpu.SemaphoreType.DMA((2,))],
        compiler_params=PARAMS,
        name="split",
    )(both)
    s1 = to_y(s0, -1)
    s3 = to_y(s0, 1)
    s2 = to_z(s0, 1)
    fm, _ = tie((fm, s0))
    fo = to_core(fm)
    s1, s3, s2, fo, mine_r = tie((s1, s3, s2, fo, mine_r))
    other_r = to_core(mine_r)
    cost = pl.CostEstimate(
        flops=KERNEL_COST, bytes_accessed=KERNEL_COST, transcendentals=0
    )
    scratch = [
        pltpu.VMEM((2048, QUART), BF),
        pltpu.VMEM((TOK, HALF), BF),
        pltpu.VMEM((TOK, HALF), BF),
        pltpu.SemaphoreType.DMA((6,)),
    ]
    um = pl.pallas_call(
        resample,
        out_shape=jax.ShapeDtypeStruct((M, QUART), F32),
        in_specs=[ANY] * 6 + [VMEM],
        out_specs=VMEM,
        scratch_shapes=scratch,
        compiler_params=PARAMS,
        cost_estimate=cost,
        name="first",
    )(mine_l, mine_r, s0, s1, s2, s3, latent_queries)
    u, packed = pl.pallas_call(
        second_kernel,
        out_shape=(
            pltpu.HBM((2, M, QUART), F32),
            pltpu.HBM((Y, 16, QUART + HEAD), BF),
        ),
        in_specs=[ANY] * 6 + [VMEM] * 4,
        out_specs=(ANY, ANY),
        scratch_shapes=scratch
        + [
            pltpu.VMEM((2, M, QUART), F32),
            pltpu.VMEM((Y, 16, QUART + HEAD), BF),
        ],
        compiler_params=PARAMS,
        cost_estimate=cost,
        name="second",
    )(other_l, other_r, s0, s1, s2, s3, latent_queries, um, fm, fo)
    arrived = lax.all_to_all(packed, "y", 0, 0, tiled=True)
    packed, t0 = tie((packed, t0))
    t1 = to_y(t0, -1)
    t3 = to_y(t0, 1)
    t2 = to_z(t0, -1)
    swapped = to_core(u)
    entered = pl.pallas_call(
        scan_kernel,
        out_shape=jax.ShapeDtypeStruct((Y, 16, QUART), BF),
        in_specs=[VMEM, ANY],
        out_specs=VMEM,
        scratch_shapes=[pltpu.VMEM((16, QUART), F32), pltpu.SemaphoreType.DMA((1,))],
        compiler_params=PARAMS,
        cost_estimate=pl.CostEstimate(
            flops=SCAN_COST, bytes_accessed=1 << 20, transcendentals=0
        ),
        name="scan",
    )(arrived, *in_hbm(init_memory[0]))
    entered, t0 = tie((entered, t0))
    queries = pl.pallas_call(
        query_kernel,
        out_shape=(pltpu.HBM((TOK, QUART), BF),) * 2,
        in_specs=[ANY] * 8,
        out_specs=(ANY, ANY),
        scratch_shapes=[pltpu.VMEM((2048, QUART), BF)]
        + [pltpu.VMEM((TOK, HALF), BF)] * 4
        + [pltpu.VMEM((TOK, QUART), BF)] * 2
        + [pltpu.SemaphoreType.DMA((8,))],
        compiler_params=PARAMS,
        cost_estimate=pl.CostEstimate(
            flops=2 * 1024 * 2048 * 512, bytes_accessed=7 << 20, transcendentals=0
        ),
        name="query",
    )(*in_hbm(mine_l, mine_r, other_l, other_r), t0, t1, t3, t2)
    e = lax.all_to_all(entered, "y", 0, 0, tiled=True).reshape(M, QUART)
    e_other = to_core(e)
    q_late, e_late = tie((queries[1], e))
    q_other = to_core(q_late)
    mixed, mem = pl.pallas_call(
        read_kernel,
        out_shape=(
            jax.ShapeDtypeStruct((TOK, HALF), BF),
            jax.ShapeDtypeStruct((M, HALF), F32),
        ),
        in_specs=[ANY] * 5 + [VMEM] * 4,
        out_specs=(VMEM, VMEM),
        scratch_shapes=[
            pltpu.VMEM((TOK, HALF), BF),
            pltpu.VMEM((TOK, QUART), BF),
            pltpu.VMEM((TOK, QUART), BF),
            pltpu.VMEM((2, M, QUART), F32),
            pltpu.VMEM((2, M, QUART), F32),
            pltpu.SemaphoreType.DMA((5,)),
        ],
        compiler_params=PARAMS,
        name="read",
    )(*in_hbm(mine_l, queries[0]), q_other, *in_hbm(u), swapped, e, e_other, fm, fo)
    return mixed[None], mem[None]


def solution(mesh):
    fine = Mesh(mesh.devices.reshape(Y, C, Z, H, L), AXES)
    seg, vid = ("y", "c"), ("z", "h")
    return jax.shard_map(
        shards,
        mesh=fine,
        in_specs=(
            P(vid, seg, "l"),
            P(vid, "l"),
            P(vid, "l"),
            P(None, "l"),
            P(vid, None, "l"),
            P(vid, seg, "l"),
        ),
        out_specs=(P(vid, seg, "l"), P(vid, seg, "l")),
        check_vma=False,
    )
```
